512 devices in a mesh: dp: 64 (over z, x_hi, core), tensor: 8 (over x_lo, y).
Axes of the slice: x: 4 (x_hi: 2, x_lo: 2; x = x_hi * 2 + x_lo), y: 4, z: 16, core: 2. Of those that a mesh axis runs over, the one named last changes fastest.
Arguments:
- gate_values: bfloat16 [8192, 14336], P('dp', 'tensor'), may hold values from -6 to 6
- up_values: bfloat16 [8192, 14336], P('dp', 'tensor'), may hold values from -6 to 6
- output_grad: bfloat16 [8192, 4096], P(('dp', 'tensor')), may hold values from -6 to 6
- kept_columns: int32 [224, 16], P('tensor'), may hold values from 0 to 63, as said below
- block_owner: int32 [224, 16], P('tensor'), may hold values from 0 to 63, as said below
- master_blocks: float32 [64, 8, 8, 4096], P('dp', 'tensor'), may hold values from -0.09375 to 0.09375
Outputs:
- layer_output: bfloat16 [8192, 4096], P(('dp', 'tensor'))
- gate_grad: bfloat16 [8192, 14336], P('dp', 'tensor')
- up_grad: bfloat16 [8192, 14336], P('dp', 'tensor')
- master_grads: float32 [64, 8, 8, 4096], P('dp', 'tensor')
The draws below stay inside these ranges and needn't reach their ends.
Inputs may be any that keep to these rules, and one draw needn't show every extreme that they name: `kept_columns`: row r lists the 16 different column blocks kept in block row r, in increasing order. `block_owner`: within one part (28 block rows), no dp index owns more than 8 blocks, and some dp index owns exactly 8.
All inputs are finite; a program needn't handle non-finite values.
Results may differ from the reference program's by a relative error of at most 0.017.
Values may be sent and summed in bfloat16 or wider, within the bound.
No kernel may reach another device: no remote copies, remote signals or barrier semaphores. Data moves between devices by JAX's collectives and lax.ppermute only.
A program may use at most 128 MiB of HBM per device.

```python
import jax
import jax.numpy as jnp
from jax import lax

D = 4096
FF = 14336
BLOCK = 64
KEEP = 16
OWNERS = 64
SLICES = 8
TOKENS = 8192
RB_T = 28
SLICE_BLOCKS = 448
CAP = 8


def draw_kept_columns(key, part):
    key = jax.random.fold_in(key, 11)
    row_keys = jax.random.split(key, FF // BLOCK)

    def one_row(row_key):
        return jnp.sort(jax.random.permutation(row_key, D // BLOCK)[:KEEP])
    return jax.vmap(one_row)(row_keys).astype(jnp.int32)


def draw_block_owner(key, part):
    key = jax.random.fold_in(key, 23)
    slice_keys = jax.random.split(key, SLICES)
    slot_total = OWNERS * CAP

    def one_slice(slice_key):
        first_key, second_key, third_key = jax.random.split(slice_key, 3)
        ordering = jax.random.permutation(first_key, slot_total)
        ranking = jnp.argsort(ordering).astype(jnp.int32)
        full_owner = jax.random.randint(second_key, (), 0, OWNERS)
        slot_ids = jnp.arange(slot_total, dtype=jnp.int32)
        priority = ranking + slot_total * (slot_ids // CAP != full_owner).astype(jnp.int32)
        chosen_slots = jnp.argsort(priority)[:SLICE_BLOCKS]
        shuffled = chosen_slots[jax.random.permutation(third_key, SLICE_BLOCKS)]
        return (shuffled // CAP).astype(jnp.int32)
    return jax.vmap(one_slice)(slice_keys).reshape(FF // BLOCK, KEEP)


def levels(rng, extent, cuts, smallest, largest):
    factor_of = 1.0
    for position, shards_of in cuts:
        draws = jax.random.uniform(jax.random.fold_in(jax.random.fold_in(rng, 6), position), (shards_of,), jnp.float32, smallest / len(cuts), largest / len(cuts))
        factor_of = factor_of * jnp.repeat(jnp.exp(draws), extent[position] // shards_of).reshape((-1,) + (1,) * (len(extent) - 1 - position))
    return factor_of


def normal_values(stream_key, extent, width, most, pieces=(), kind=jnp.bfloat16):
    level = levels(stream_key, extent, pieces, -0.22, 0.18) if pieces else 1.0
    values = jax.random.normal(stream_key, extent, jnp.float32) * width * level
    return jnp.minimum(jnp.maximum(values, -most), most).astype(kind)


def setup_inputs(seed: int = 0) -> dict:
    splits = jax.random.split(jax.random.key(seed), 7)
    return {
        "gate_values": normal_values(splits[0], (TOKENS, FF), 1.0, 6.0, ((0, 64), (1, 8))),
        "up_values": normal_values(splits[1], (TOKENS, FF), 1.0, 6.0, ((0, 64), (1, 8))),
        "output_grad": normal_values(splits[2], (TOKENS, D), 1.0, 6.0, ((0, 512),)),
        "kept_columns": draw_kept_columns(jax.random.fold_in(splits[6], 71), 0),
        "block_owner": draw_block_owner(jax.random.fold_in(splits[6], 71), 0),
        "master_blocks": normal_values(splits[5], (OWNERS, SLICES, CAP, BLOCK * BLOCK), (FF // 4) ** -0.5, 0.09375, ((0, 64), (1, 8)), jnp.float32),
    }


def slot_ranks(owner_list, owner_count):
    flat_owner = owner_list.reshape(-1)
    owner_ids = jnp.arange(owner_count, dtype=jnp.int32)
    membership = (flat_owner[:, None] == owner_ids[None, :]).astype(jnp.int32)
    earlier = jnp.cumsum(membership, axis=0) - membership
    return jnp.sum(earlier * membership, axis=1).astype(jnp.int32)


def reference(gate_values, up_values, output_grad, kept_columns, block_owner, master_blocks):
    gate_wide = gate_values.astype(jnp.float32)
    up_wide = up_values.astype(jnp.float32)
    sigmoid_gate = jax.nn.sigmoid(gate_wide)
    swish_gate = gate_wide * sigmoid_gate
    hidden = (swish_gate * up_wide).astype(jnp.bfloat16)
    row_total = FF // BLOCK
    col_total = D // BLOCK
    owner_slices = block_owner.reshape(SLICES, SLICE_BLOCKS)
    slot_rank = jax.vmap(lambda grid: slot_ranks(grid, OWNERS))(owner_slices)
    slice_ids = jnp.broadcast_to(jnp.arange(SLICES, dtype=jnp.int32)[:, None], (SLICES, SLICE_BLOCKS))
    picked = master_blocks[owner_slices, slice_ids, slot_rank]
    rounded = lax.optimization_barrier(picked.astype(jnp.bfloat16))
    weights = rounded.astype(jnp.float32).reshape(row_total, KEEP, BLOCK, BLOCK)
    hidden_blocks = hidden.astype(jnp.float32).reshape(TOKENS, row_total, BLOCK)
    grad_blocks = output_grad.astype(jnp.float32).reshape(TOKENS, col_total, BLOCK)

    def slice_pass(summed, slice_index):
        def row_pass(partial_value, row_index):
            global_row = slice_index * RB_T + row_index
            row_cols = lax.dynamic_index_in_dim(kept_columns, global_row, 0, keepdims=False)
            row_weights = lax.dynamic_index_in_dim(weights, global_row, 0, keepdims=False)
            row_hidden = lax.dynamic_index_in_dim(hidden_blocks, global_row, 1, keepdims=False)
            chosen = jnp.take(grad_blocks, row_cols, axis=1)
            forward = jnp.einsum("ti,kij->tkj", row_hidden, row_weights)
            partial_value = partial_value.at[:, row_cols].add(forward)
            backward = jnp.einsum("tkj,kij->ti", chosen, row_weights)
            local = jnp.einsum("ti,tkj->kij", row_hidden, chosen)
            return partial_value, (backward, local)

        start = jnp.zeros((TOKENS, col_total, BLOCK), jnp.float32)
        partial_value, outputs = lax.scan(row_pass, start, jnp.arange(RB_T, dtype=jnp.int32))
        part_round = lax.optimization_barrier(partial_value.astype(jnp.bfloat16))
        summed = summed + part_round.astype(jnp.float32)
        return summed, outputs

    zeros_out = jnp.zeros((TOKENS, col_total, BLOCK), jnp.float32)
    summed, (backward, local) = lax.scan(slice_pass, zeros_out, jnp.arange(SLICES, dtype=jnp.int32))
    layer_output = summed.reshape(TOKENS, D).astype(jnp.bfloat16)
    hidden_grad = jnp.transpose(backward, (2, 0, 1, 3)).reshape(TOKENS, FF)
    up_grad = (hidden_grad * swish_gate).astype(jnp.bfloat16)
    gate_grad = (hidden_grad * up_wide * sigmoid_gate * (1.0 + gate_wide * (1.0 - sigmoid_gate))).astype(jnp.bfloat16)
    block_grads = local.reshape(SLICES, SLICE_BLOCKS, BLOCK * BLOCK) * (TOKENS ** -0.5)
    master_grads = jnp.zeros((OWNERS, SLICES, CAP, BLOCK * BLOCK), jnp.float32)
    master_grads = master_grads.at[owner_slices, slice_ids, slot_rank].set(block_grads)
    return layer_output, gate_grad, up_grad, master_grads
```

```python
import jax
import jax.numpy as jnp
import numpy as np
from jax import lax
from jax.experimental import pallas as pl
from jax.experimental.pallas import tpu as pltpu
from jax.sharding import Mesh, PartitionSpec as P

BLOCK = 64
HALF = 32
LANES = 128


def grads_kernel(cols, places, gate, up, grad, packed, wide):
    row_count, width = grad.shape
    kept = 16
    packed[...] = jnp.zeros_like(packed)

    def turn(pair, carry):
        columns = pl.ds(pl.multiple_of(pair * LANES, LANES), LANES)
        turned = grad[:, columns].T
        for side in range(2):
            for part in range(2):
                first = side * BLOCK + part * HALF
                wide[2 * pair + side, :, part * row_count : (part + 1) * row_count] = turned[
                    first : first + HALF
                ]
        return carry

    lax.fori_loop(0, width // LANES, turn, 0)
    lane = lax.broadcasted_iota(jnp.int32, (row_count, LANES), 1)

    def rows(pair, carry):
        columns = pl.ds(pl.multiple_of(pair * LANES, LANES), LANES)
        gate_wide = gate[:, columns].astype(jnp.float32)
        hidden = gate_wide * jax.nn.sigmoid(gate_wide) * up[:, columns].astype(jnp.float32)
        swapped = pltpu.roll(hidden, BLOCK, 1)
        for side in range(2):
            low, high = (hidden, swapped) if side == 0 else (swapped, hidden)
            spread = jnp.concatenate(
                [jnp.where(lane < BLOCK, low, 0.0), jnp.where(lane < BLOCK, 0.0, high)], axis=0
            ).astype(jnp.bfloat16)
            first = (2 * pair + side) * kept
            chosen = jnp.concatenate([wide[cols[first + k]] for k in range(kept)], axis=0)
            result = jnp.dot(chosen, spread, preferred_element_type=jnp.float32)
            result = result.astype(jnp.bfloat16)
            for k in range(kept):
                packed[places[first + k]] = result[k * HALF : (k + 1) * HALF]
        return carry

    lax.fori_loop(0, gate.shape[1] // LANES, rows, 0)


def passes_kernel(cols, places, gate, up, grad, blocks, out, gate_grad, up_grad, dense, hidden):
    row_count, width = grad.shape
    units = gate.shape[1]
    kept = 16
    lane = lax.broadcasted_iota(jnp.int32, (HALF, LANES), 1)

    def clear(step, carry):
        dense[pl.ds(pl.multiple_of(step * BLOCK, BLOCK), BLOCK), :] = jnp.zeros((BLOCK, units), jnp.bfloat16)
        return carry

    lax.fori_loop(0, width // BLOCK, clear, 0)

    def fill(pair, carry):
        columns = pl.ds(pl.multiple_of(pair * LANES, LANES), LANES)
        gate_wide = gate[:, columns].astype(jnp.float32)
        hidden[:, columns] = (
            gate_wide * jax.nn.sigmoid(gate_wide) * up[:, columns].astype(jnp.float32)
        ).astype(jnp.bfloat16)
        for side in range(2):
            mine = (lane < BLOCK) if side == 0 else (lane >= BLOCK)
            for k in range(kept):
                spot = (2 * pair + side) * kept + k
                block = blocks[places[spot]].astype(jnp.float32)
                swapped = pltpu.roll(block, BLOCK, 1)
                pieces = (block, swapped) if side == 0 else (swapped, block)
                first = cols[spot] * BLOCK
                for part in range(2):
                    there = pl.ds(pl.multiple_of(first + part * HALF, HALF), HALF)
                    old = dense[there, columns].astype(jnp.float32)
                    dense[there, columns] = jnp.where(mine, pieces[part], old).astype(jnp.bfloat16)
        return carry

    lax.fori_loop(0, units // LANES, fill, 0)
    step = 256

    def forward(turn, carry):
        columns = pl.ds(pl.multiple_of(turn * step, step), step)
        out[:, columns] = lax.dot_general(
            hidden[...], dense[columns, :], (((1,), (1,)), ((), ())), preferred_element_type=jnp.float32
        ).astype(out.dtype)
        return carry

    lax.fori_loop(0, width // step, forward, 0)

    def backward(turn, carry):
        columns = pl.ds(pl.multiple_of(turn * step, step), step)
        hidden_grad = jnp.dot(grad[...], dense[:, columns], preferred_element_type=jnp.float32)
        gate_wide = gate[:, columns].astype(jnp.float32)
        sigmoid_gate = jax.nn.sigmoid(gate_wide)
        up_grad[:, columns] = (hidden_grad * (gate_wide * sigmoid_gate)).astype(up_grad.dtype)
        gate_grad[:, columns] = (
            hidden_grad
            * up[:, columns].astype(jnp.float32)
            * sigmoid_gate
            * (1.0 + gate_wide * (1.0 - sigmoid_gate))
        ).astype(gate_grad.dtype)
        return carry

    lax.fori_loop(0, units // step, backward, 0)


def block_grads(cols, places, gate, up, grad, slots):
    rows, width = grad.shape
    return pl.pallas_call(
        grads_kernel,
        out_shape=jax.ShapeDtypeStruct((slots, HALF, LANES), jnp.bfloat16),
        grid_spec=pltpu.PrefetchScalarGridSpec(
            num_scalar_prefetch=2,
            grid=(),
            in_specs=[pl.BlockSpec(memory_space=pltpu.VMEM)] * 3,
            out_specs=pl.BlockSpec(memory_space=pltpu.VMEM),
            scratch_shapes=[pltpu.VMEM((width // BLOCK, HALF, 2 * rows), jnp.bfloat16)],
        ),
        compiler_params=pltpu.CompilerParams(vmem_limit_bytes=32 * 2**20),
        cost_estimate=pl.CostEstimate(flops=4 * 10**9, bytes_accessed=7 * 2**20, transcendentals=0),
        name="block_grads",
    )(cols, places, gate, up, grad)


def both_passes(cols, places, gate, up, grad, blocks):
    rows, width = grad.shape
    units = gate.shape[1]
    like = jax.ShapeDtypeStruct((rows, units), jnp.bfloat16)
    return pl.pallas_call(
        passes_kernel,
        out_shape=(jax.ShapeDtypeStruct((rows, width), jnp.bfloat16), like, like),
        grid_spec=pltpu.PrefetchScalarGridSpec(
            num_scalar_prefetch=2,
            grid=(),
            in_specs=[pl.BlockSpec(memory_space=pltpu.VMEM)] * 4,
            out_specs=[pl.BlockSpec(memory_space=pltpu.VMEM)] * 3,
            scratch_shapes=[
                pltpu.VMEM((width, units), jnp.bfloat16),
                pltpu.VMEM((rows, units), jnp.bfloat16),
            ],
        ),
        compiler_params=pltpu.CompilerParams(vmem_limit_bytes=48 * 2**20),
        cost_estimate=pl.CostEstimate(flops=4 * 10**9, bytes_accessed=8 * 2**20, transcendentals=0),
        name="both_passes",
    )(cols, places, gate, up, grad, blocks)


def swap(x, axis):
    return lax.ppermute(x, axis, [(0, 1), (1, 0)])


def on_device(gate_values, up_values, output_grad, kept_columns, block_owner, master_blocks):
    capacity, square = master_blocks.shape[2:]
    depth, flanks, cores = (lax.axis_size(name) for name in ("z", "x_hi", "core"))
    parts = lax.axis_size(("x_lo", "y"))
    slots = depth * flanks * cores * capacity
    row_count = output_grad.shape[0] * parts
    width = output_grad.shape[1]
    core, flank = lax.axis_index("core"), lax.axis_index("x_hi")

    stored = master_blocks.reshape(capacity, BLOCK, 2, HALF).astype(jnp.bfloat16)
    stored = stored.transpose(0, 3, 2, 1).reshape(capacity, HALF, LANES)
    beside = swap(stored, "x_hi")
    pair = jnp.where(flank == 0, jnp.stack([stored, beside]), jnp.stack([beside, stored]))
    column = lax.all_gather(pair, "z", axis=0, tiled=False)
    other = swap(column, "core")
    arrived = jnp.stack([column, other]).reshape(slots, HALF, LANES)

    full_grad = lax.all_to_all(
        jnp.broadcast_to(output_grad[None], (parts,) + output_grad.shape),
        ("x_lo", "y"), split_axis=0, concat_axis=0, tiled=True,
    ).reshape(row_count, width)

    owner = block_owner.reshape(-1)
    index = jnp.arange(owner.shape[0], dtype=jnp.int32)
    same = (owner[:, None] == owner[None, :]) & (index[None, :] < index[:, None])
    slot_rank = jnp.sum(same.astype(jnp.int32), axis=1)
    owner_core = owner % cores
    within = (owner // cores) * capacity + slot_rank
    half = slots // cores
    cols = kept_columns.reshape(-1)
    grads = block_grads(cols, owner_core * half + within, gate_values, up_values, full_grad, slots)
    grads = grads.reshape(cores, half, HALF, LANES)
    kept = lax.dynamic_index_in_dim(grads, core, 0, keepdims=False)
    sent = lax.dynamic_index_in_dim(grads, 1 - core, 0, keepdims=False)
    chip = (kept.astype(jnp.float32) + swap(sent, "core").astype(jnp.float32)).astype(jnp.bfloat16)
    chip = chip.reshape(depth, flanks, capacity, HALF, LANES)
    line = lax.psum_scatter(chip, "z", scatter_dimension=0, tiled=False)
    kept = lax.dynamic_index_in_dim(line, flank, 0, keepdims=False)
    sent = lax.dynamic_index_in_dim(line, 1 - flank, 0, keepdims=False)
    total = kept.astype(jnp.float32) + swap(sent, "x_hi").astype(jnp.float32)
    token_count = row_count * depth * flanks * cores
    total = total * float(token_count) ** (-0.5)
    master_grads = (
        total.reshape(capacity, HALF, 2, BLOCK).transpose(0, 3, 2, 1).reshape(1, 1, capacity, square)
    )

    here = (owner_core != core).astype(jnp.int32) * half + within
    partial_out, gate_grad, up_grad = both_passes(
        cols, here, gate_values, up_values, full_grad, arrived
    )
    shares = lax.all_to_all(
        partial_out.reshape(parts, row_count // parts, width),
        ("x_lo", "y"), split_axis=0, concat_axis=0, tiled=True,
    )
    layer_output = jnp.sum(shares.astype(jnp.float32), axis=0).astype(jnp.bfloat16)
    return layer_output, gate_grad, up_grad, master_grads


def solution(mesh):
    fine = Mesh(mesh.devices.reshape(16, 2, 2, 2, 4), ("z", "x_hi", "core", "x_lo", "y"))
    dp, tensor = ("z", "x_hi", "core"), ("x_lo", "y")
    return jax.shard_map(
        on_device,
        mesh=fine,
        in_specs=(
            P(dp, tensor),
            P(dp, tensor),
            P(dp + tensor, None),
            P(tensor, None),
            P(tensor, None),
            P(dp, tensor, None, None),
        ),
        out_specs=(
            P(dp + tensor, None),
            P(dp, tensor),
            P(dp, tensor),
            P(dp, tensor, None, None),
        ),
        check_vma=False,
    )
```

```python
import jax
import jax.numpy as jnp
import numpy as np
from jax import lax
from jax.experimental import pallas as pl
from jax.experimental.pallas import tpu as pltpu
from jax.sharding import Mesh, PartitionSpec as P

BLOCK = 64
HALF = 32
LANES = 128
Z = ("z_hi", "z_lo")


def grads_kernel(cols, places, gate_far, up_far, grad, packed, wide, gate, up, arrivals):
    row_count, width = grad.shape
    kept = 16
    copies = [
        pltpu.make_async_copy(gate_far, gate, arrivals.at[0]),
        pltpu.make_async_copy(up_far, up, arrivals.at[1]),
    ]
    for copy in copies:
        copy.start()
    packed[...] = jnp.zeros_like(packed)

    def turn(pair, carry):
        columns = pl.ds(pl.multiple_of(pair * LANES, LANES), LANES)
        turned = grad[:, columns].T
        for side in range(2):
            for part in range(2):
                first = side * BLOCK + part * HALF
                wide[2 * pair + side, :, part * row_count : (part + 1) * row_count] = turned[
                    first : first + HALF
                ]
        return carry

    lax.fori_loop(0, width // LANES, turn, 0, unroll=32)
    for copy in copies:
        copy.wait()
    lane = lax.broadcasted_iota(jnp.int32, (row_count, LANES), 1)

    def rows(pair, carry):
        columns = pl.ds(pl.multiple_of(pair * LANES, LANES), LANES)
        gate_wide = gate[:, columns].astype(jnp.float32)
        hidden = gate_wide * jax.nn.sigmoid(gate_wide) * up[:, columns].astype(jnp.float32)
        swapped = pltpu.roll(hidden, BLOCK, 1)
        for side in range(2):
            low, high = (hidden, swapped) if side == 0 else (swapped, hidden)
            spread = jnp.concatenate(
                [jnp.where(lane < BLOCK, low, 0.0), jnp.where(lane < BLOCK, 0.0, high)], axis=0
            ).astype(jnp.bfloat16)
            first = (2 * pair + side) * kept
            chosen = jnp.concatenate([wide[cols[first + k]] for k in range(kept)], axis=0)
            result = jnp.dot(chosen, spread, preferred_element_type=jnp.float32)
            result = result.astype(jnp.bfloat16)
            for k in range(kept):
                packed[places[first + k]] = result[k * HALF : (k + 1) * HALF]
        return carry

    lax.fori_loop(0, gate.shape[1] // LANES, rows, 0, unroll=14)


def passes_kernel(
    cols, places, gate, up, wide, *refs
):
    *pieces, out, gate_grad, up_grad, sums, blocks, arrivals = refs
    row_count = gate.shape[0]
    kept = 16
    copies, first = [], 0
    for index, piece in enumerate(pieces):
        there = blocks.at[pl.ds(first, piece.shape[0])]
        copies.append(pltpu.make_async_copy(piece, there, arrivals.at[index]))
        first += piece.shape[0]
    for copy in copies:
        copy.start()

    def clear(index, carry):
        sums[index] = jnp.zeros(sums.shape[1:], jnp.float32)
        return carry

    lax.fori_loop(0, sums.shape[0], clear, 0, unroll=8)
    for copy in copies:
        copy.wait()
    empty = jnp.zeros((BLOCK, row_count), jnp.bfloat16)

    def rows(pair, carry):
        columns = pl.ds(pl.multiple_of(pair * LANES, LANES), LANES)
        gate_wide = gate[:, columns].astype(jnp.float32)
        up_wide = up[:, columns].astype(jnp.float32)
        sigmoid_gate = jax.nn.sigmoid(gate_wide)
        swish_gate = gate_wide * sigmoid_gate
        turned = (swish_gate * up_wide).T.astype(jnp.bfloat16)
        halves = []
        for side in range(2):
            mine = turned[side * BLOCK : (side + 1) * BLOCK]
            spread = jnp.concatenate(
                [jnp.concatenate([mine, empty], axis=1), jnp.concatenate([empty, mine], axis=1)], axis=0
            )
            first = (2 * pair + side) * kept
            weights = jnp.concatenate([blocks[places[first + k]] for k in range(kept)], axis=0)
            forward = jnp.dot(weights, spread, preferred_element_type=jnp.float32)
            for start in range(0, kept, 4):
                group = range(start, start + 4)
                old = [sums[cols[first + k]] for k in group]
                for k in group:
                    sums[cols[first + k]] = old[k - start] + forward[k * HALF : (k + 1) * HALF]
            chosen = jnp.concatenate([wide[cols[first + k]] for k in range(kept)], axis=0)
            backward = lax.dot_general(
                weights, chosen, (((0,), (0,)), ((), ())), preferred_element_type=jnp.float32
            )
            halves.append(backward[:BLOCK, :row_count] + backward[BLOCK:, row_count:])
        hidden_grad = jnp.concatenate(halves, axis=0).T
        up_grad[:, columns] = (hidden_grad * swish_gate).astype(up_grad.dtype)
        gate_grad[:, columns] = (
            hidden_grad * up_wide * sigmoid_gate * (1.0 + gate_wide * (1.0 - sigmoid_gate))
        ).astype(gate_grad.dtype)
        return carry

    lax.fori_loop(0, gate.shape[1] // LANES, rows, 0, unroll=14)

    def close(pair, carry):
        columns = pl.ds(pl.multiple_of(pair * LANES, LANES), LANES)
        tall = jnp.concatenate(
            [
                sums[2 * pair + side][:, part * row_count : (part + 1) * row_count]
                for side in range(2)
                for part in range(2)
            ],
            axis=0,
        )
        out[:, columns] = tall.T.astype(out.dtype)
        return carry

    lax.fori_loop(0, sums.shape[0] // 2, close, 0, unroll=32)


def block_grads(cols, places, gate, up, grad, slots):
    rows, width = grad.shape
    return pl.pallas_call(
        grads_kernel,
        out_shape=(
            jax.ShapeDtypeStruct((slots, HALF, LANES), jnp.bfloat16),
            jax.ShapeDtypeStruct((width // BLOCK, HALF, 2 * rows), jnp.bfloat16),
        ),
        grid_spec=pltpu.PrefetchScalarGridSpec(
            num_scalar_prefetch=2,
            grid=(),
            in_specs=[pl.BlockSpec(memory_space=pl.ANY)] * 2 + [pl.BlockSpec(memory_space=pltpu.VMEM)],
            out_specs=[pl.BlockSpec(memory_space=pltpu.VMEM)] * 2,
            scratch_shapes=[pltpu.VMEM(gate.shape, gate.dtype), pltpu.VMEM(up.shape, up.dtype), pltpu.SemaphoreType.DMA((2,))],
        ),
        compiler_params=pltpu.CompilerParams(vmem_limit_bytes=32 * 2**20),
        cost_estimate=pl.CostEstimate(flops=9 * 10**9, bytes_accessed=7 * 2**20, transcendentals=0),
        name="block_grads",
    )(cols, places, gate, up, grad)


def both_passes(cols, places, gate, up, wide, *pieces):
    rows, units = gate.shape
    col_blocks = wide.shape[0]
    like = jax.ShapeDtypeStruct((rows, units), jnp.bfloat16)
    return pl.pallas_call(
        passes_kernel,
        out_shape=(jax.ShapeDtypeStruct((rows, col_blocks * BLOCK), jnp.bfloat16), like, like),
        grid_spec=pltpu.PrefetchScalarGridSpec(
            num_scalar_prefetch=2,
            grid=(),
            in_specs=[pl.BlockSpec(memory_space=pltpu.VMEM)] * 3 + [pl.BlockSpec(memory_space=pl.ANY)] * len(pieces),
            out_specs=[pl.BlockSpec(memory_space=pltpu.VMEM)] * 3,
            scratch_shapes=[
                pltpu.VMEM((col_blocks, HALF, 2 * rows), jnp.float32),
                pltpu.VMEM((sum(piece.shape[0] for piece in pieces), HALF, LANES), jnp.bfloat16),
                pltpu.SemaphoreType.DMA((len(pieces),)),
            ],
        ),
        compiler_params=pltpu.CompilerParams(vmem_limit_bytes=32 * 2**20),
        cost_estimate=pl.CostEstimate(flops=10**6, bytes_accessed=2**16, transcendentals=0),
        name="both_passes",
    )(cols, places, gate, up, wide, *pieces)


def swap(x, axis):
    return lax.ppermute(x, axis, [(0, 1), (1, 0)])


def after(x, *others):
    return lax.optimization_barrier((x,) + others)[0]


def add_up(x, y):
    return (x.astype(jnp.float32) + y.astype(jnp.float32)).astype(jnp.bfloat16)


def on_device(gate_values, up_values, output_grad, kept_columns, block_owner, master_blocks):
    capacity, square = master_blocks.shape[2:]
    depth, flanks, cores = (lax.axis_size(name) for name in (Z, "x_hi", "core"))
    parts = lax.axis_size(("x_lo", "y"))
    slots = depth * flanks * cores * capacity
    row_count = output_grad.shape[0] * parts
    width = output_grad.shape[1]
    core, flank = lax.axis_index("core"), lax.axis_index("x_hi")

    stored = master_blocks.reshape(capacity, BLOCK, 2, HALF).astype(jnp.bfloat16)
    stored = stored.transpose(0, 3, 2, 1).reshape(capacity, HALF, LANES)
    copies = jnp.broadcast_to(output_grad[None], (parts,) + output_grad.shape)
    full_grad = lax.all_to_all(
        copies, ("x_lo", "y"), split_axis=0, concat_axis=0, tiled=True
    ).reshape(row_count, width)
    stored = after(stored, copies)
    away = depth // 2
    across = [((z * 2 + x), ((z + away) % depth) * 2 + 1 - x) for z in range(depth) for x in range(2)]
    shift = lambda x, by: lax.ppermute(x, Z, [(z, (z + by) % depth) for z in range(depth)])
    firsts = [stored, swap(stored, "x_hi"), shift(stored, away), lax.ppermute(stored, Z + ("x_hi",), across)]
    own = jnp.concatenate(firsts)

    owner = block_owner.reshape(-1)
    index = jnp.arange(owner.shape[0], dtype=jnp.int32)
    same = (owner[:, None] == owner[None, :]) & (index[None, :] < index[:, None])
    slot_rank = jnp.sum(same.astype(jnp.int32), axis=1)
    owner_core = owner % cores
    owner_flank = (owner // cores) % flanks
    owner_depth = owner // (cores * flanks)
    far_core = (owner_core != core).astype(jnp.int32)
    far_flank = (owner_flank != flank).astype(jnp.int32)
    cols = kept_columns.reshape(-1)
    spots = ((far_core * depth + owner_depth) * flanks + far_flank) * capacity + slot_rank
    grads, wide = block_grads(cols, spots, gate_values, up_values, after(full_grad, *firsts), slots)
    grads = grads.reshape(cores, depth, flanks, capacity, HALF, LANES)
    chip = add_up(grads[0], swap(grads[1], "core"))
    line = lax.psum_scatter(chip, Z, scatter_dimension=0, tiled=False)
    total = line[0].astype(jnp.float32) + swap(line[1], "x_hi").astype(jnp.float32)
    own = after(own, chip)
    ups, downs, rise, fall = [], [], own, own
    for hop in range(1, away // 2):
        rise, fall = shift(rise, -1), shift(fall, 1)
        ups.append(rise)
        downs.append(fall)
    last = 2 * capacity
    near = jnp.concatenate([own] + ups + downs + [shift(rise[:last], -1), shift(fall[:last], 1)])
    far = swap(near, "core")
    ahead = (owner_depth - lax.axis_index(Z)) % depth
    ahead_slot = [0] * depth
    for hop in range(1, away // 2):
        ahead_slot[hop], ahead_slot[hop + away] = 4 * hop, 4 * hop + 2
        back = 4 * (away // 2 - 1 + hop)
        ahead_slot[depth - hop], ahead_slot[away - hop] = back, back + 2
    ahead_slot[away] = 2
    ahead_slot[away // 2] = 4 * (away - 1)
    ahead_slot[depth - away // 2] = 4 * (away - 1) + 2
    piece = jnp.asarray(np.array(ahead_slot, np.int32))[ahead] + far_flank
    here = far_core * (depth * flanks * capacity) + piece * capacity + slot_rank
    token_count = row_count * depth * flanks * cores
    total = total * float(token_count) ** (-0.5)
    master_grads = (
        total.reshape(capacity, HALF, 2, BLOCK).transpose(0, 3, 2, 1).reshape(1, 1, capacity, square)
    )
    partial_out, gate_grad, up_grad = both_passes(
        cols, here, gate_values, up_values, wide, near, far
    )
    shares = lax.all_to_all(
        partial_out.reshape(parts, row_count // parts, width),
        ("x_lo", "y"), split_axis=0, concat_axis=0, tiled=True,
    )
    layer_output = jnp.sum(shares.astype(jnp.float32), axis=0).astype(jnp.bfloat16)
    return layer_output, gate_grad, up_grad, master_grads


def solution(mesh):
    fine = Mesh(mesh.devices.reshape(4, 4, 2, 2, 2, 4), ("z_hi", "z_lo", "x_hi", "core", "x_lo", "y"))
    dp, tensor = Z + ("x_hi", "core"), ("x_lo", "y")
    return jax.shard_map(
        on_device,
        mesh=fine,
        in_specs=(
            P(dp, tensor),
            P(dp, tensor),
            P(dp + tensor, None),
            P(tensor, None),
            P(tensor, None),
            P(dp, tensor, None, None),
        ),
        out_specs=(
            P(dp + tensor, None),
            P(dp, tensor),
            P(dp, tensor),
            P(dp, tensor, None, None),
        ),
        check_vma=False,
    )
```

```python
import jax
import jax.numpy as jnp
import numpy as np
from jax import lax
from jax.experimental import pallas as pl
from jax.experimental.pallas import tpu as pltpu
from jax.sharding import Mesh, PartitionSpec as P

BLOCK = 64
HALF = 32
LANES = 128
Z = ("z_hi", "z_lo")


def grads_kernel(cols, places, gate_far, up_far, grad, packed, wide, gate, up, arrivals):
    row_count, width = grad.shape
    kept = 16
    copies = [
        pltpu.make_async_copy(gate_far, gate, arrivals.at[0]),
        pltpu.make_async_copy(up_far, up, arrivals.at[1]),
    ]
    for copy in copies:
        copy.start()
    packed[...] = jnp.zeros_like(packed)

    def turn(pair, carry):
        columns = pl.ds(pl.multiple_of(pair * LANES, LANES), LANES)
        turned = grad[:, columns].T
        for side in range(2):
            for part in range(2):
                first = side * BLOCK + part * HALF
                wide[2 * pair + side, :, part * row_count : (part + 1) * row_count] = turned[
                    first : first + HALF
                ]
        return carry

    lax.fori_loop(0, width // LANES, turn, 0, unroll=32)
    for copy in copies:
        copy.wait()
    lane = lax.broadcasted_iota(jnp.int32, (row_count, LANES), 1)

    def rows(pair, carry):
        columns = pl.ds(pl.multiple_of(pair * LANES, LANES), LANES)
        gate_wide = gate[:, columns].astype(jnp.float32)
        hidden = gate_wide * jax.nn.sigmoid(gate_wide) * up[:, columns].astype(jnp.float32)
        swapped = pltpu.roll(hidden, BLOCK, 1)
        for side in range(2):
            low, high = (hidden, swapped) if side == 0 else (swapped, hidden)
            spread = jnp.concatenate(
                [jnp.where(lane < BLOCK, low, 0.0), jnp.where(lane < BLOCK, 0.0, high)], axis=0
            ).astype(jnp.bfloat16)
            first = (2 * pair + side) * kept
            chosen = jnp.concatenate([wide[cols[first + k]] for k in range(kept)], axis=0)
            result = jnp.dot(chosen, spread, preferred_element_type=jnp.float32)
            result = result.astype(jnp.bfloat16)
            for k in range(kept):
                packed[places[first + k]] = result[k * HALF : (k + 1) * HALF]
        return carry

    lax.fori_loop(0, gate.shape[1] // LANES, rows, 0, unroll=14)


def passes_kernel(
    cols, places, gate, up, wide, *refs
):
    *pieces, out, gate_grad, up_grad, sums, blocks, arrivals = refs
    row_count = gate.shape[0]
    kept = 16
    copies, first = [], 0
    for index, piece in enumerate(pieces):
        there = blocks.at[pl.ds(first, piece.shape[0])]
        copies.append(pltpu.make_async_copy(piece, there, arrivals.at[index]))
        first += piece.shape[0]
    for copy in copies:
        copy.start()

    def clear(index, carry):
        sums[index] = jnp.zeros(sums.shape[1:], jnp.float32)
        return carry

    lax.fori_loop(0, sums.shape[0], clear, 0, unroll=8)
    for copy in copies:
        copy.wait()
    empty = jnp.zeros((BLOCK, row_count), jnp.bfloat16)

    def rows(pair, carry):
        columns = pl.ds(pl.multiple_of(pair * LANES, LANES), LANES)
        gate_wide = gate[:, columns].astype(jnp.float32)
        up_wide = up[:, columns].astype(jnp.float32)
        sigmoid_gate = jax.nn.sigmoid(gate_wide)
        swish_gate = gate_wide * sigmoid_gate
        turned = (swish_gate * up_wide).T.astype(jnp.bfloat16)
        halves = []
        for side in range(2):
            mine = turned[side * BLOCK : (side + 1) * BLOCK]
            spread = jnp.concatenate(
                [jnp.concatenate([mine, empty], axis=1), jnp.concatenate([empty, mine], axis=1)], axis=0
            )
            first = (2 * pair + side) * kept
            weights = jnp.concatenate([blocks[places[first + k]] for k in range(kept)], axis=0)
            forward = jnp.dot(weights, spread, preferred_element_type=jnp.float32)
            for start in range(0, kept, 4):
                group = range(start, start + 4)
                old = [sums[cols[first + k]] for k in group]
                for k in group:
                    sums[cols[first + k]] = old[k - start] + forward[k * HALF : (k + 1) * HALF]
            chosen = jnp.concatenate([wide[cols[first + k]] for k in range(kept)], axis=0)
            backward = lax.dot_general(
                weights, chosen, (((0,), (0,)), ((), ())), preferred_element_type=jnp.float32
            )
            halves.append(backward[:BLOCK, :row_count] + backward[BLOCK:, row_count:])
        hidden_grad = jnp.concatenate(halves, axis=0).T
        up_grad[:, columns] = (hidden_grad * swish_gate).astype(up_grad.dtype)
        gate_grad[:, columns] = (
            hidden_grad * up_wide * sigmoid_gate * (1.0 + gate_wide * (1.0 - sigmoid_gate))
        ).astype(gate_grad.dtype)
        return carry

    lax.fori_loop(0, gate.shape[1] // LANES, rows, 0, unroll=14)

    def close(pair, carry):
        columns = pl.ds(pl.multiple_of(pair * LANES, LANES), LANES)
        tall = jnp.concatenate(
            [
                sums[2 * pair + side][:, part * row_count : (part + 1) * row_count]
                for side in range(2)
                for part in range(2)
            ],
            axis=0,
        )
        out[:, columns] = tall.T.astype(out.dtype)
        return carry

    lax.fori_loop(0, sums.shape[0] // 2, close, 0, unroll=32)


def block_grads(cols, places, gate, up, grad, slots):
    rows, width = grad.shape
    return pl.pallas_call(
        grads_kernel,
        out_shape=(
            jax.ShapeDtypeStruct((slots, HALF, LANES), jnp.bfloat16),
            jax.ShapeDtypeStruct((width // BLOCK, HALF, 2 * rows), jnp.bfloat16),
        ),
        grid_spec=pltpu.PrefetchScalarGridSpec(
            num_scalar_prefetch=2,
            grid=(),
            in_specs=[pl.BlockSpec(memory_space=pl.ANY)] * 2 + [pl.BlockSpec(memory_space=pltpu.VMEM)],
            out_specs=[pl.BlockSpec(memory_space=pltpu.VMEM)] * 2,
            scratch_shapes=[pltpu.VMEM(gate.shape, gate.dtype), pltpu.VMEM(up.shape, up.dtype), pltpu.SemaphoreType.DMA((2,))],
        ),
        compiler_params=pltpu.CompilerParams(vmem_limit_bytes=32 * 2**20),
        cost_estimate=pl.CostEstimate(flops=9 * 10**9, bytes_accessed=7 * 2**20, transcendentals=0),
        name="block_grads",
    )(cols, places, gate, up, grad)


def both_passes(cols, places, gate, up, wide, *pieces):
    rows, units = gate.shape
    col_blocks = wide.shape[0]
    like = jax.ShapeDtypeStruct((rows, units), jnp.bfloat16)
    return pl.pallas_call(
        passes_kernel,
        out_shape=(jax.ShapeDtypeStruct((rows, col_blocks * BLOCK), jnp.bfloat16), like, like),
        grid_spec=pltpu.PrefetchScalarGridSpec(
            num_scalar_prefetch=2,
            grid=(),
            in_specs=[pl.BlockSpec(memory_space=pltpu.VMEM)] * 3 + [pl.BlockSpec(memory_space=pl.ANY)] * len(pieces),
            out_specs=[pl.BlockSpec(memory_space=pltpu.VMEM)] * 3,
            scratch_shapes=[
                pltpu.VMEM((col_blocks, HALF, 2 * rows), jnp.float32),
                pltpu.VMEM((sum(piece.shape[0] for piece in pieces), HALF, LANES), jnp.bfloat16),
                pltpu.SemaphoreType.DMA((len(pieces),)),
            ],
        ),
        compiler_params=pltpu.CompilerParams(vmem_limit_bytes=32 * 2**20),
        cost_estimate=pl.CostEstimate(flops=10**6, bytes_accessed=2**16, transcendentals=0),
        name="both_passes",
    )(cols, places, gate, up, wide, *pieces)


def swap(x, axis):
    return lax.ppermute(x, axis, [(0, 1), (1, 0)])


def after(x, *others):
    return lax.optimization_barrier((x,) + others)[0]


def add_up(x, y):
    return (x.astype(jnp.float32) + y.astype(jnp.float32)).astype(jnp.bfloat16)


def on_device(gate_values, up_values, output_grad, kept_columns, block_owner, master_blocks):
    capacity, square = master_blocks.shape[2:]
    depth, flanks, cores = (lax.axis_size(name) for name in (Z, "x_hi", "core"))
    parts = lax.axis_size(("x_lo", "y"))
    slots = depth * flanks * cores * capacity
    row_count = output_grad.shape[0] * parts
    width = output_grad.shape[1]
    core, flank = lax.axis_index("core"), lax.axis_index("x_hi")

    stored = master_blocks.reshape(capacity, BLOCK, 2, HALF).astype(jnp.bfloat16)
    stored = stored.transpose(0, 3, 2, 1).reshape(capacity, HALF, LANES)
    copies = jnp.broadcast_to(output_grad[None], (parts,) + output_grad.shape)
    full_grad = lax.all_to_all(
        copies, ("x_lo", "y"), split_axis=0, concat_axis=0, tiled=True
    ).reshape(row_count, width)
    away = depth // 2
    across = [((z * 2 + x), ((z + away) % depth) * 2 + 1 - x) for z in range(depth) for x in range(2)]
    shift = lambda x, by: lax.ppermute(x, Z, [(z, (z + by) % depth) for z in range(depth)])
    firsts = [stored, swap(stored, "x_hi"), shift(stored, away), lax.ppermute(stored, Z + ("x_hi",), across)]
    own = jnp.concatenate(firsts)

    owner = block_owner.reshape(-1)
    index = jnp.arange(owner.shape[0], dtype=jnp.int32)
    same = (owner[:, None] == owner[None, :]) & (index[None, :] < index[:, None])
    slot_rank = jnp.sum(same.astype(jnp.int32), axis=1)
    owner_core = owner % cores
    owner_flank = (owner // cores) % flanks
    owner_depth = owner // (cores * flanks)
    far_core = (owner_core != core).astype(jnp.int32)
    far_flank = (owner_flank != flank).astype(jnp.int32)
    cols = kept_columns.reshape(-1)
    spots = ((far_core * depth + owner_depth) * flanks + far_flank) * capacity + slot_rank
    grads, wide = block_grads(cols, spots, gate_values, up_values, after(full_grad, *firsts), slots)
    grads = grads.reshape(cores, depth, flanks, capacity, HALF, LANES)
    chip = add_up(grads[0], swap(grads[1], "core"))
    line = lax.psum_scatter(chip, Z, scatter_dimension=0, tiled=False)
    total = line[0].astype(jnp.float32) + swap(line[1], "x_hi").astype(jnp.float32)
    own = after(own, chip)
    ups, downs, rise, fall = [], [], own, own
    for hop in range(1, away // 2):
        rise, fall = shift(rise, -1), shift(fall, 1)
        ups.append(rise)
        downs.append(fall)
    last = 2 * capacity
    near = jnp.concatenate([own] + ups + downs + [shift(rise[:last], -1), shift(fall[:last], 1)])
    far = swap(near, "core")
    ahead = (owner_depth - lax.axis_index(Z)) % depth
    ahead_slot = [0] * depth
    for hop in range(1, away // 2):
        ahead_slot[hop], ahead_slot[hop + away] = 4 * hop, 4 * hop + 2
        back = 4 * (away // 2 - 1 + hop)
        ahead_slot[depth - hop], ahead_slot[away - hop] = back, back + 2
    ahead_slot[away] = 2
    ahead_slot[away // 2] = 4 * (away - 1)
    ahead_slot[depth - away // 2] = 4 * (away - 1) + 2
    piece = jnp.asarray(np.array(ahead_slot, np.int32))[ahead] + far_flank
    here = far_core * (depth * flanks * capacity) + piece * capacity + slot_rank
    token_count = row_count * depth * flanks * cores
    total = total * float(token_count) ** (-0.5)
    master_grads = (
        total.reshape(capacity, HALF, 2, BLOCK).transpose(0, 3, 2, 1).reshape(1, 1, capacity, square)
    )
    partial_out, gate_grad, up_grad = both_passes(
        cols, here, gate_values, up_values, wide, near, far
    )
    shares = lax.all_to_all(
        partial_out.reshape(parts, row_count // parts, width),
        ("x_lo", "y"), split_axis=0, concat_axis=0, tiled=True,
    )
    layer_output = jnp.sum(shares.astype(jnp.float32), axis=0).astype(jnp.bfloat16)
    return layer_output, gate_grad, up_grad, master_grads


def solution(mesh):
    fine = Mesh(mesh.devices.reshape(4, 4, 2, 2, 2, 4), ("z_hi", "z_lo", "x_hi", "core", "x_lo", "y"))
    dp, tensor = Z + ("x_hi", "core"), ("x_lo", "y")
    return jax.shard_map(
        on_device,
        mesh=fine,
        in_specs=(
            P(dp, tensor),
            P(dp, tensor),
            P(dp + tensor, None),
            P(tensor, None),
            P(tensor, None),
            P(dp, tensor, None, None),
        ),
        out_specs=(
            P(dp + tensor, None),
            P(dp, tensor),
            P(dp, tensor),
            P(dp, tensor, None, None),
        ),
        check_vma=False,
    )
```
